512 devices in a mesh: dp: 32 (over z, y_lo), mp: 16 (over x, y_hi, core).
Axes of the slice: x: 4, y: 4 (y_hi: 2, y_lo: 2; y = y_hi * 2 + y_lo), z: 16, core: 2. Of those that a mesh axis runs over, the one named last changes fastest.
Arguments:
- inputs: bfloat16 [8192, 16384], P('dp', 'mp'), may hold values from -6 to 6
- grad_out: bfloat16 [8192, 16384], P('dp', 'mp'), may hold values from -6 to 6
- up_first: bfloat16 [128, 128, 128], P('mp'), may hold values from -6 to 6
- up_second: bfloat16 [128, 128, 512], P('mp'), may hold values from -6 to 6
- down_first: bfloat16 [128, 512, 128], P('mp'), may hold values from -6 to 6
- down_second: bfloat16 [128, 128, 128], P('mp'), may hold values from -6 to 6
- dither_first: int32 [128, 128, 128], P('mp', 'dp'), may hold values from 0 to 32767
- dither_second: int32 [128, 128, 512], P('mp', 'dp'), may hold values from 0 to 32767
- dither_third: int32 [128, 512, 128], P('mp', 'dp'), may hold values from 0 to 32767
- dither_fourth: int32 [128, 128, 128], P('mp', 'dp'), may hold values from 0 to 32767
Outputs:
- grad_inputs: bfloat16 [8192, 16384], P('dp', 'mp')
- new_up_first: bfloat16 [128, 128, 128], P('mp', 'dp')
- new_up_second: bfloat16 [128, 128, 512], P('mp', 'dp')
- new_down_first: bfloat16 [128, 512, 128], P('mp', 'dp')
- new_down_second: bfloat16 [128, 128, 128], P('mp', 'dp')
The draws below stay inside these ranges and needn't reach their ends.
Inputs may be any that keep to these rules, and one draw needn't show every extreme that they name: `dither_first`: random bits, one per weight element. `dither_second`: random bits, one per weight element. `dither_third`: random bits, one per weight element. `dither_fourth`: random bits, one per weight element.
All inputs are finite; a program needn't handle non-finite values.
Results may differ from the reference program's by a relative error of at most 0.01.
Values may be sent and summed in bfloat16 or wider, within the bound.
No kernel may reach another device: no remote copies, remote signals or barrier semaphores. Data moves between devices by JAX's collectives and lax.ppermute only.
A program may use at most 64 MiB of HBM per device.

```python
import math
import jax
import jax.numpy as jnp
from jax import lax

BLOCK_COUNT = 128
TILE_SPAN = 128
HB = 512
TOK_DEV = 256
D = 16384
TOKENS = 8192
N_DP = 32


def place_ends(result, key, low, largest):
    place = [jax.random.randint(jax.random.fold_in(key, axis), (), 0, length) for axis, length in enumerate(result.shape)]
    main_axis = result.shape.index(max(result.shape))
    beside = place[:main_axis] + [(place[main_axis] + 1) % result.shape[main_axis]] + place[main_axis + 1:]
    return result.at[tuple(place)].set(low).at[tuple(beside)].set(largest)


def block_levels(stream_key, shape, cuts, smallest, top_value):
    def one(axis_at, blocks):
        steps = jax.random.uniform(jax.random.fold_in(jax.random.fold_in(stream_key, 6), axis_at), (blocks,), jnp.float32, smallest / len(cuts), top_value / len(cuts))
        return jnp.repeat(jnp.exp(steps), shape[axis_at] // blocks).reshape((-1,) + (1,) * (len(shape) - axis_at - 1))

    factor_of = one(*cuts[0])
    for cut in cuts[1:]:
        factor_of = factor_of * one(*cut)
    return factor_of


def scatter_about(own_key, extent, width, limit, pieces=(), kind=jnp.bfloat16):
    factor_of = block_levels(own_key, extent, pieces, -0.22, 0.18) if pieces else 1.0
    array = jax.random.normal(own_key, extent, jnp.float32) * width * factor_of
    return jnp.minimum(jnp.maximum(array, -limit), limit).astype(kind)


def setup_inputs(seed: int = 0) -> dict:
    key_list = jax.random.split(jax.random.key(seed), 11)
    return {
        "inputs": scatter_about(key_list[0], (TOKENS, D), 1.0, 6.0, ((0, 32), (1, 16))),
        "grad_out": scatter_about(key_list[1], (TOKENS, D), 1.0, 6.0, ((0, 32), (1, 16))),
        "up_first": scatter_about(key_list[2], (BLOCK_COUNT, TILE_SPAN, BLOCK_COUNT), 1.0, 6.0, ((0, 16),)),
        "up_second": scatter_about(key_list[3], (BLOCK_COUNT, BLOCK_COUNT, HB), 1.0, 6.0, ((0, 16),)),
        "down_first": scatter_about(key_list[4], (BLOCK_COUNT, HB, BLOCK_COUNT), 1.0, 6.0, ((0, 16),)),
        "down_second": scatter_about(key_list[5], (BLOCK_COUNT, BLOCK_COUNT, TILE_SPAN), 1.0, 6.0, ((0, 16),)),
        "dither_first": place_ends(jax.random.randint(key_list[6], (BLOCK_COUNT, TILE_SPAN, BLOCK_COUNT), 0, 32768), jax.random.fold_in(key_list[6], 1), 0, 32767).astype(jnp.int32),
        "dither_second": place_ends(jax.random.randint(key_list[7], (BLOCK_COUNT, BLOCK_COUNT, HB), 0, 32768), jax.random.fold_in(key_list[7], 1), 0, 32767).astype(jnp.int32),
        "dither_third": place_ends(jax.random.randint(key_list[8], (BLOCK_COUNT, HB, BLOCK_COUNT), 0, 32768), jax.random.fold_in(key_list[8], 1), 0, 32767).astype(jnp.int32),
        "dither_fourth": place_ends(jax.random.randint(key_list[9], (BLOCK_COUNT, BLOCK_COUNT, TILE_SPAN), 0, 32768), jax.random.fold_in(key_list[9], 1), 0, 32767).astype(jnp.int32),
    }


grid_step = 0.25

def noisy_quantized_matrix(value):
    return lax.optimization_barrier(value.astype(jnp.bfloat16)).astype(jnp.float32)

def gelu_back(preactivation, dgated):
    return jax.vjp(jax.nn.gelu, preactivation)[1](dgated)[0]

def passes(rows, cotangent, leading_matrix_entries, second_factor_weight, weight_three, weight_four):
    count = rows.shape[0]
    tile_partition = rows.reshape(count, BLOCK_COUNT, TILE_SPAN).astype(jnp.float32)
    leading_monarch_matrix = noisy_quantized_matrix(jnp.einsum('gma,mad->gmd', tile_partition, leading_matrix_entries) * TILE_SPAN ** (-0.5))
    preactivation = jnp.einsum('dqs,sqa->dsa', leading_monarch_matrix, second_factor_weight) * BLOCK_COUNT ** (-0.5)
    gated = noisy_quantized_matrix(jax.nn.gelu(preactivation))
    down = noisy_quantized_matrix(jnp.einsum('tmc,mck->tmk', gated, weight_three) * HB ** (-0.5))
    cot_blocks = cotangent.reshape(count, BLOCK_COUNT, TILE_SPAN).astype(jnp.float32)
    grad_four = jnp.einsum('tmk,tkj->kmj', down, cot_blocks) * BLOCK_COUNT ** (-0.5)
    back_down = noisy_quantized_matrix(jnp.einsum('tkj,kmj->tkm', cot_blocks, weight_four) * BLOCK_COUNT ** (-0.5))
    grad_three = jnp.einsum('tmc,tkm->mck', gated, back_down) * HB ** (-0.5)
    dgated = jnp.einsum('tkm,mck->tmc', back_down, weight_three) * HB ** (-0.5)
    preactivation_gradient = noisy_quantized_matrix(gelu_back(preactivation, dgated))
    gradient_factor_second = jnp.einsum('pfx,pxv->xfv', leading_monarch_matrix, preactivation_gradient) * BLOCK_COUNT ** (-0.5)
    incoming_cotangent_signal = noisy_quantized_matrix(jnp.einsum('aev,ewv->awe', preactivation_gradient, second_factor_weight) * BLOCK_COUNT ** (-0.5))
    gradient_factor_first = jnp.einsum('aew,aed->ewd', tile_partition, incoming_cotangent_signal) * TILE_SPAN ** (-0.5)
    sensitivity_line_entries = (jnp.einsum('knv,nmv->knm', incoming_cotangent_signal, leading_matrix_entries) * TILE_SPAN ** (-0.5)).astype(jnp.bfloat16)
    return (sensitivity_line_entries.reshape(count, BLOCK_COUNT * TILE_SPAN), (gradient_factor_first, gradient_factor_second, grad_three, grad_four))

def updated(weight, grad_sum, dither, rate):
    noise = grid_step * (dither.astype(jnp.float32) / 32768.0 - 0.5)
    return (weight.astype(jnp.float32) - rate * grad_sum + noise).astype(jnp.bfloat16)

def reference(inputs, grad_out, up_first, up_second, down_first, down_second, dither_first, dither_second, dither_third, dither_fourth):
    weights = (up_first.astype(jnp.float32), up_second.astype(jnp.float32), down_first.astype(jnp.float32), down_second.astype(jnp.float32))

    def group(carry, index):
        start = (index * TOK_DEV).astype(jnp.int32)
        rows = lax.dynamic_slice_in_dim(inputs, start, TOK_DEV, 0)
        cotangent = lax.dynamic_slice_in_dim(grad_out, start, TOK_DEV, 0)
        sensitivity_line_entries, grads = passes(rows, cotangent, weights[0], weights[1], weights[2], weights[3])
        carry = tuple((total + noisy_quantized_matrix(part) for total, part in zip(carry, grads)))
        return (carry, sensitivity_line_entries)
    start_sums = tuple((jnp.zeros(w.shape, jnp.float32) for w in weights))
    sums, grad_groups = lax.scan(group, start_sums, jnp.arange(N_DP, dtype=jnp.int32))
    grad_inputs = grad_groups.reshape(TOKENS, BLOCK_COUNT * TILE_SPAN)
    rate = 4.0 / math.sqrt(TOKENS)
    new_one = updated(up_first, sums[0], dither_first, rate)
    new_two = updated(up_second, sums[1], dither_second, rate)
    new_three = updated(down_first, sums[2], dither_third, rate)
    new_four = updated(down_second, sums[3], dither_fourth, rate)
    return (grad_inputs, new_one, new_two, new_three, new_four)
```

```python
import math

import jax
import jax.numpy as jnp
from jax import lax
from jax.sharding import Mesh, PartitionSpec as P

TILE = 128
HB = 512
GRID = 0.25
BF = jnp.bfloat16
F32 = jnp.float32

DP = ("zh", "zl", "yl")
MP = ("mp",)
SUB = ("zl", "yl")
FAR = ("zh",)
GROUP = SUB + MP


def dot(spec, a, b, scale):
    return jnp.einsum(spec, a, b, preferred_element_type=F32) * scale


def exchange(a, axes):
    return lax.all_to_all(a, axes, 0, 0, tiled=True)


def gelu_back(pre, dgated):
    return jax.vjp(jax.nn.gelu, pre)[1](dgated)[0]


def updated(weight, grad_sum, dither):
    rows = dither.shape[1]
    start = lax.axis_index(DP) * rows
    own = lax.dynamic_slice_in_dim(weight, start, rows, 1).astype(F32)
    rate = 4.0 / math.sqrt(8192)
    noise = GRID * (dither.astype(F32) / 32768.0 - 0.5)
    return (own - rate * grad_sum + noise).astype(BF)


def on_device(x, dy, up1, up2, dn1, dn2, di1, di2, di3, di4):
    T = x.shape[0]
    NB = up1.shape[0]
    NS = lax.axis_size(SUB)
    NG = lax.axis_size(MP)
    NZ = lax.axis_size(FAR)
    ML = NB // NS
    s1 = TILE ** -0.5
    s5 = HB ** -0.5
    xb = x.reshape(T, NB, TILE)
    yb = dy.reshape(T, NB, TILE)
    first = dot("tbi,bim->mbt", xb, up1, s1).astype(BF)
    back_down = dot("tkj,kmj->mkt", yb, dn2, s1).astype(BF)
    both = jnp.concatenate([first, back_down], 1)
    both = both.reshape(NG, NS, ML, 2 * NB, T).transpose(1, 0, 2, 3, 4)
    got = exchange(both.reshape(NS * NG, ML, 2 * NB, T), GROUP)
    got = got.reshape(NS, NG, ML, 2, NB, T)
    fm = got[:, :, :, 0].transpose(2, 1, 3, 0, 4).reshape(ML, TILE, NS * T)
    bd = got[:, :, :, 1].transpose(2, 1, 3, 0, 4).reshape(ML, TILE, NS * T)
    sub = lax.axis_index(SUB)
    w2 = lax.dynamic_slice_in_dim(up2, sub * ML, ML, 0)
    w3 = lax.dynamic_slice_in_dim(dn1, sub * ML, ML, 0)
    pre = dot("mbt,mbc->mct", fm, w2, s1)
    gated = jax.nn.gelu(pre).astype(BF)
    down = dot("mct,mck->mkt", gated, w3, s5).astype(BF)
    grad3 = dot("mct,mkt->mck", gated, bd, s5)
    dgated = dot("mkt,mck->mct", bd, w3, s5)
    dpre = gelu_back(pre, dgated).astype(BF)
    grad2 = dot("mbt,mct->mbc", fm, dpre, s1)
    back_up = dot("mct,mbc->mbt", dpre, w2, s1).astype(BF)
    g2 = grad2.astype(BF).reshape(ML, NZ, TILE // NZ, HB).transpose(1, 0, 2, 3)
    g3 = grad3.astype(BF).reshape(ML, NZ, HB // NZ, TILE).transpose(1, 0, 2, 3)
    g23 = jnp.concatenate([g2.reshape(NZ, -1), g3.reshape(NZ, -1)], 1).reshape(NZ, 1, -1, 128)
    r23 = lax.psum_scatter(g23, FAR, scatter_dimension=0, tiled=True)
    send = jnp.stack([down, back_up], 1)
    send = send.reshape(ML, 2, NG, NB, NS, T).transpose(4, 2, 0, 1, 3, 5)
    R = TILE // (NZ * NS)

    def tail(send, xb, yb, up1):
        got = exchange(send.reshape(NS * NG, ML, 2 * NB, T), GROUP)
        got = got.reshape(NS, NG, ML, 2, NB, T)
        dn = got[:, :, :, 0].transpose(3, 1, 0, 2, 4).reshape(NB, TILE, T)
        bu = got[:, :, :, 1].transpose(3, 1, 0, 2, 4).reshape(NB, TILE, T)
        grad4 = dot("kmt,tkj->kmj", dn, yb, s1)
        grad1 = dot("tbi,bmt->bim", xb, bu, s1)
        g14 = jnp.stack([grad1, grad4]).astype(BF)
        g14 = g14.reshape(2, NB, NZ, NS, R, TILE).transpose(3, 2, 0, 1, 4, 5)
        g14 = exchange(g14.reshape(NS, NZ, 2, NB * R, TILE), SUB)
        return bu, jnp.sum(g14.astype(F32), 0).astype(BF)

    def never(send, xb, yb, up1):
        return jnp.zeros((NB, TILE, T), BF), jnp.zeros((NZ, 2, NB * R, TILE), BF)

    bu, g14 = lax.cond(lax.axis_index("mp") < 999, tail, never, send, xb, yb, up1)
    g14, r23, bu = lax.optimization_barrier((g14, r23, bu))
    gin = dot("bmt,bim->tbi", bu, up1, s1).astype(BF).reshape(T, NB * TILE)
    g14 = exchange(g14, FAR)
    g14 = jnp.sum(g14.astype(F32), 0)
    sum1 = g14[0].reshape(NB, R, TILE)
    sum4 = g14[1].reshape(NB, R, TILE)
    n2 = ML * (TILE // NZ) * HB
    r23 = r23.reshape(-1)
    r2 = r23[:n2].reshape(ML, NS, R, HB).transpose(1, 0, 2, 3).reshape(NS, -1)
    r3 = r23[n2:].reshape(ML, NS, R * 4, TILE).transpose(1, 0, 2, 3).reshape(NS, -1)
    q = jnp.concatenate([r2, r3], 1).reshape(NS, -1, 128)
    mine = lax.dynamic_index_in_dim(q, sub, 0, keepdims=False)
    outs = [mine]
    for k in range(1, NS):
        outs.append(lax.ppermute(lax.dynamic_index_in_dim(q, sub ^ k, 0, keepdims=False), SUB, [(i, i ^ k) for i in range(NS)]))
    q = jnp.stack(outs)
    q = jnp.take(q, sub ^ jnp.arange(NS), axis=0).astype(F32).reshape(NS, -1)
    h = q.shape[1] // 2
    sum2 = q[:, :h].reshape(NB, R, HB)
    sum3 = q[:, h:].reshape(NB, R * 4, TILE)
    return (
        gin,
        updated(up1, sum1, di1),
        updated(up2, sum2, di2),
        updated(dn1, sum3, di3),
        updated(dn2, sum4, di4),
    )


def solution(mesh):
    dp, mp = mesh.shape["dp"], mesh.shape["mp"]
    fine = Mesh(mesh.devices.reshape(dp // 4, 2, 2, mp), ("zh", "zl", "yl", "mp"))
    w = P("mp", None, None)
    d = P("mp", DP, None)
    return jax.shard_map(
        on_device,
        mesh=fine,
        in_specs=(P(DP, "mp"), P(DP, "mp"), w, w, w, w, d, d, d, d),
        out_specs=(P(DP, "mp"), d, d, d, d),
        check_vma=False,
    )
```

```python
import math

import jax
import jax.numpy as jnp
from jax import lax
from jax.experimental import pallas as pl
from jax.experimental.pallas import tpu as pltpu
from jax.sharding import Mesh, PartitionSpec as P

TILE = 128
HB = 512
T = 256
NB = 8
NS = 4
NG = 16
NZ = 8
NQ = 4
ML = NB // NS
R = TILE // (NZ * NS)
GRID = 0.25
RATE = 4.0 / math.sqrt(8192)
S1 = TILE ** -0.5
S5 = HB ** -0.5
C0 = math.sqrt(2.0 / math.pi)
BF = jnp.bfloat16
F32 = jnp.float32

DP = ("z3", "zq", "zl", "yl")
SUB = ("zl", "yl")
FAR = ("z3", "zq")
GROUP = SUB + ("mp",)

NN = (((1,), (0,)), ((), ()))
NT = (((1,), (1,)), ((), ()))
TN = (((0,), (0,)), ((), ()))
TT = (((0,), (1,)), ((), ()))
PARAMS = pltpu.CompilerParams(vmem_limit_bytes=48 << 20)
ALL_VMEM = pltpu.CompilerParams(vmem_limit_bytes=60 << 20)


def mm(a, b, dims):
    return lax.dot_general(a, b, dims, preferred_element_type=F32)


def exchange(a, axes):
    return lax.all_to_all(a, axes, 0, 0, tiled=True)


def cost(flops, moved):
    return pl.CostEstimate(flops=flops, bytes_accessed=moved, transcendentals=0)


def first_kernel(x, u, y, d, out, rows):
    for h in range(2):
        t = slice(h * 128, (h + 1) * 128)
        for b in range(NB):
            f = slice(b * TILE, (b + 1) * TILE)
            rows[h, pl.ds(b, TILE, stride=2 * NB), :] = mm(u[b], x[t, f], TT) * S1
            rows[h, pl.ds(NB + b, TILE, stride=2 * NB), :] = mm(d[b], y[t, f], NT) * S1
    for h in range(2):
        v = rows[h].reshape(NG, NS, 2 * NB * ML, 128).astype(BF)
        for s in range(NS):
            out[s * NG : (s + 1) * NG, :, h * 128 : (h + 1) * 128] = v[:, s]


def first_stage(x, u, y, d):
    return pl.pallas_call(
        first_kernel,
        out_shape=jax.ShapeDtypeStruct((NS * NG, 2 * NB * ML, T), BF),
        scratch_shapes=[pltpu.VMEM((2, TILE * 2 * NB, 128), F32)],
        compiler_params=ALL_VMEM,
        cost_estimate=cost(2**27, 2**21),
    )(x, u, y, d)


def hidden_kernel(at, r, w2, w3, out, p0, p1, p2, p3, cut):
    w2 = w2[0]
    w3 = w3[0]
    g2 = g3 = None
    for s in range(NS):
        v = r[s * NG : (s + 1) * NG].astype(F32)
        fm = v[:, :NB].reshape(TILE, T).astype(BF)
        bd = v[:, NB:].reshape(TILE, T).astype(BF)
        pre = mm(w2, fm, TN) * S1
        dgated = mm(w3, bd, NN) * S5
        th = jnp.tanh(C0 * (pre + 0.044715 * (pre * pre * pre)))
        cdf = 0.5 * (1.0 + th)
        gated = (pre * cdf).astype(BF)
        slope = cdf + (0.5 * C0) * pre * (1.0 - th * th) * (1.0 + (3 * 0.044715) * (pre * pre))
        dpre = (dgated * slope).astype(BF)
        down = mm(w3, gated, TN) * S5
        back_up = mm(w2, dpre, NN) * S1
        a2 = mm(fm, dpre, NT)
        a3 = mm(gated, bd, NT)
        g2, g3 = (a2, a3) if g2 is None else (g2 + a2, g3 + a3)
        both = jnp.concatenate([down.reshape(NG, NB, T), back_up.reshape(NG, NB, T)], 1)
        out[s * NG : (s + 1) * NG] = both.astype(BF)
    for c in range(4):
        v = (g2[:, c * 128 : (c + 1) * 128] * S1).reshape(NZ, NS, R, 128)
        for s in range(NS):
            cut[:, s, c * R : (c + 1) * R] = v[:, s]
    cut[:, :, 4 * R :] = (g3 * S5).reshape(NZ, NS, 4 * R, 128)
    for k, p in enumerate((p0, p1, p2, p3)):
        for h in range(2):
            p[h * NS : (h + 1) * NS] = cut[h * NQ + (at[1] ^ k)].astype(BF)


def hidden_stage(at, r, up2, dn1):
    spec = pltpu.PrefetchScalarGridSpec(
        num_scalar_prefetch=1,
        grid=(ML,),
        in_specs=[
            pl.BlockSpec((NS * NG, 2 * NB, T), lambda m, s: (0, m, 0)),
            pl.BlockSpec((1, TILE, HB), lambda m, s: (s[2] * ML + m, 0, 0)),
            pl.BlockSpec((1, HB, TILE), lambda m, s: (s[2] * ML + m, 0, 0)),
        ],
        out_specs=[pl.BlockSpec((NS * NG, 2 * NB, T), lambda m, s: (0, m, 0))]
        + [pl.BlockSpec((2 * NS, 8 * R, 128), lambda m, s: (0, m, 0))] * NQ,
        scratch_shapes=[pltpu.VMEM((NZ, NS, 8 * R, 128), F32)],
    )
    return pl.pallas_call(
        hidden_kernel,
        grid_spec=spec,
        out_shape=[jax.ShapeDtypeStruct((NS * NG, 2 * NB * ML, T), BF)]
        + [jax.ShapeDtypeStruct((2 * NS, 8 * R * ML, 128), BF)] * NQ,
        compiler_params=PARAMS,
        cost_estimate=cost(2**30, 2**22),
    )(at, r, up2, dn1)


def outer_kernel(r, x, y, u, p0, p1, p2, p3, gin, grads, rows, cut):
    for s in range(NS):
        for h in range(2):
            rows[h, :, s] = r[s * NG : (s + 1) * NG, :, h * 128 : (h + 1) * 128].astype(F32)
    flat = rows.reshape(2, TILE * 2 * NB, 128)

    def pick(j):
        return jnp.concatenate([flat[h, pl.ds(j, TILE, stride=2 * NB), :] for h in range(2)], 1).astype(BF)

    for b in range(NB):
        f = slice(b * TILE, (b + 1) * TILE)
        down, back_up = pick(b), pick(NB + b)
        gin[:, f] = (mm(back_up, u[b], TT) * S1).astype(BF)
        g1 = (mm(x[:, f], back_up, TT) * S1).reshape(NZ, NS, R, TILE)
        g4 = (mm(down, y[:, f], NN) * S1).reshape(NZ, NS, R, TILE)
        for s in range(NS):
            cut[s, :, b * R : (b + 1) * R] = g1[:, s]
            cut[s, :, (NB + b) * R : (NB + b + 1) * R] = g4[:, s]
    grads[:, :NZ] = cut[...].astype(BF)
    g23 = (p0[...].astype(F32) + p1[...].astype(F32)) + (p2[...].astype(F32) + p3[...].astype(F32))
    g23 = g23.astype(BF)
    for h in range(2):
        grads[:, NZ + h] = g23[h * NS : (h + 1) * NS]


def outer_stage(r, x, y, u, p):
    return pl.pallas_call(
        outer_kernel,
        out_shape=[
            jax.ShapeDtypeStruct((T, NB * TILE), BF),
            jax.ShapeDtypeStruct((NS, NZ + 2, 2 * NB * R, TILE), BF),
        ],
        scratch_shapes=[
            pltpu.VMEM((2, NG, NS, 2 * NB * ML, 128), F32),
            pltpu.VMEM((NS, NZ, 2 * NB * R, TILE), F32),
        ],
        compiler_params=PARAMS,
        cost_estimate=cost(2**10, 2**10),
    )(r, x, y, u, *p)


def near_kernel(at, a, g14, keep, give):
    v = a[0, :NZ].astype(F32)
    for s in range(1, NS):
        v = v + a[s, :NZ].astype(F32)
    g14[...] = v.astype(BF)
    keep[...] = a[:, NZ + at[0]]
    give[...] = a[:, NZ + 1 - at[0]]


def near_stage(at, a):
    return pl.pallas_call(
        near_kernel,
        in_specs=[pl.BlockSpec(memory_space=pltpu.SMEM), pl.BlockSpec(memory_space=pltpu.VMEM)],
        out_shape=[
            jax.ShapeDtypeStruct((NZ, 2 * NB * R, TILE), BF),
            jax.ShapeDtypeStruct((NS, 8 * R * ML, 128), BF),
            jax.ShapeDtypeStruct((NS, 8 * R * ML, 128), BF),
        ],
        compiler_params=PARAMS,
        cost_estimate=cost(2**10, 2**10),
    )(at, a)


def choose(sub, options):
    v = options[-1]
    for s in range(len(options) - 2, -1, -1):
        v = jnp.where(sub == s, options[s], v)
    return v


def step(weight, grad, dither):
    noise = GRID * (dither.astype(F32) / 32768.0 - 0.5)
    return (weight - RATE * grad + noise).astype(BF)


def own_rows(sub, block):
    v = block.astype(F32)
    return choose(sub, [v[:, s * R : (s + 1) * R] for s in range(NS)])


def update_kernel(at, a, keep, took, up1, up2, dn1, dn2, d1, d2, d3, d4, n1, n2, n3, n4):
    sub = at[2]
    v = a[0].astype(F32)
    for z in range(1, NZ):
        v = v + a[z].astype(F32)
    g = v.reshape(2, NB, R, TILE)
    n1[...] = step(own_rows(sub, up1[...]), g[0], d1[...])
    n4[...] = step(own_rows(sub, dn2[...]), g[1], d4[...])
    own = own_rows(sub, up2[...])
    for s in range(NS):
        v = keep[s].astype(F32) + took[s].astype(F32)
        for i in range(ML):
            m = s * ML + i
            w = v[i * 8 * R : (i + 1) * 8 * R]
            grad = jnp.concatenate([w[c * R : (c + 1) * R] for c in range(4)], 1)
            n2[m] = step(own[m], grad, d2[m])
            n3[m] = step(dn1[m].astype(F32), w[4 * R :], d3[m])


def update(at, a, keep, took, up1, up2, dn1, dn2, d1, d2, d3, d4):
    def whole(*shape):
        return pl.BlockSpec(shape, lambda i, s: (0,) * len(shape))

    def far(s):
        return s[0] * NQ + s[1]

    small = whole(NB, R, TILE)
    wide = whole(NB, R, HB)
    large = whole(NB, 4 * R, TILE)
    half = whole(NS, 8 * R * ML, 128)
    block = pl.BlockSpec((NB, NS * R, TILE), lambda i, s: (0, far(s), 0))
    spec = pltpu.PrefetchScalarGridSpec(
        num_scalar_prefetch=1,
        grid=(1,),
        in_specs=[
            whole(NZ, 2 * NB * R, TILE),
            half,
            half,
            block,
            pl.BlockSpec((NB, NS * R, HB), lambda i, s: (0, far(s), 0)),
            pl.BlockSpec((NB, 4 * R, TILE), lambda i, s: (0, far(s) * NS + s[2], 0)),
            block,
            small,
            wide,
            large,
            small,
        ],
        out_specs=[small, wide, large, small],
    )
    shapes = ((NB, R, TILE), (NB, R, HB), (NB, 4 * R, TILE), (NB, R, TILE))
    return pl.pallas_call(
        update_kernel,
        grid_spec=spec,
        out_shape=[jax.ShapeDtypeStruct(shape, BF) for shape in shapes],
        compiler_params=PARAMS,
        cost_estimate=cost(2**10, 2**10),
    )(at, a, keep, took, up1, up2, dn1, dn2, d1, d2, d3, d4)


def on_device(x, dy, up1, up2, dn1, dn2, di1, di2, di3, di4):
    at = jnp.stack([lax.axis_index(a) for a in ("z3", "zq", SUB)]).astype(jnp.int32)
    always = lax.axis_index("mp") < 999

    def fenced(a, axes):
        return lax.cond(always, lambda a: exchange(a, axes), jnp.zeros_like, a)

    got = exchange(first_stage(x, up1, dy, dn2), GROUP)
    send, *p = hidden_stage(at, got, up2, dn1)
    p = [p[0]] + [lax.ppermute(p[k], "zq", [(i, i ^ k) for i in range(NQ)]) for k in range(1, NQ)]
    got, p = lax.optimization_barrier((fenced(send, GROUP), p))
    gin, grads = outer_stage(got, x, dy, up1, p)
    g14, keep, give = near_stage(at, exchange(grads, SUB))
    took = lax.ppermute(give, "z3", [(0, 1), (1, 0)])
    g14, took = lax.optimization_barrier((fenced(g14, FAR), took))
    new1, new2, new3, new4 = update(at, g14, keep, took, up1, up2, dn1, dn2, di1, di2, di3, di4)
    return gin, new1, new2, new3, new4


def solution(mesh):
    dp, mp = mesh.shape["dp"], mesh.shape["mp"]
    fine = Mesh(mesh.devices.reshape(2, dp // 8, 2, 2, mp), ("z3", "zq", "zl", "yl", "mp"))
    w = P("mp", None, None)
    d = P("mp", DP, None)
    return jax.shard_map(
        on_device,
        mesh=fine,
        in_specs=(P(DP, "mp"), P(DP, "mp"), w, w, w, w, d, d, d, d),
        out_specs=(P(DP, "mp"), d, d, d, d),
        check_vma=False,
    )
```

```python
import math

import jax
import jax.numpy as jnp
from jax import lax
from jax.experimental import pallas as pl
from jax.experimental.pallas import tpu as pltpu
from jax.sharding import Mesh, PartitionSpec as P

TILE = 128
HB = 512
T = 256
NB = 8
NS = 4
NG = 16
NZ = 8
NQ = 4
ML = NB // NS
R = TILE // (NZ * NS)
GRID = 0.25
RATE = 4.0 / math.sqrt(8192)
S1 = TILE ** -0.5
S5 = HB ** -0.5
C0 = math.sqrt(2.0 / math.pi)
BF = jnp.bfloat16
F32 = jnp.float32

DP = ("fq", "z1", "zl", "yl")
SUB = ("zl", "yl")
FAR = ("fq", "z1")
GROUP = SUB + ("mp",)

NN = (((1,), (0,)), ((), ()))
NT = (((1,), (1,)), ((), ()))
TN = (((0,), (0,)), ((), ()))
TT = (((0,), (1,)), ((), ()))
PARAMS = pltpu.CompilerParams(vmem_limit_bytes=48 << 20)
FULL = pltpu.CompilerParams(vmem_limit_bytes=64 << 20)
ALL_VMEM = pltpu.CompilerParams(vmem_limit_bytes=60 << 20)


def mm(a, b, dims):
    return lax.dot_general(a, b, dims, preferred_element_type=F32)


def exchange(a, axes):
    return lax.all_to_all(a, axes, 0, 0, tiled=True)


def cost(flops, moved):
    return pl.CostEstimate(flops=flops, bytes_accessed=moved, transcendentals=0)


def first_kernel(x, u, y, d, out, rows):
    for h in range(2):
        t = slice(h * 128, (h + 1) * 128)
        for b in range(NB):
            f = slice(b * TILE, (b + 1) * TILE)
            rows[h, pl.ds(b, TILE, stride=2 * NB), :] = mm(u[b], x[t, f], TT) * S1
            rows[h, pl.ds(NB + b, TILE, stride=2 * NB), :] = mm(d[b], y[t, f], NT) * S1
    for h in range(2):
        v = rows[h].reshape(NG, NS, 2 * NB * ML, 128).astype(BF)
        for s in range(NS):
            out[s * NG : (s + 1) * NG, :, h * 128 : (h + 1) * 128] = v[:, s]


def first_stage(x, u, y, d):
    return pl.pallas_call(
        first_kernel,
        out_shape=jax.ShapeDtypeStruct((NS * NG, 2 * NB * ML, T), BF),
        scratch_shapes=[pltpu.VMEM((2, TILE * 2 * NB, 128), F32)],
        compiler_params=ALL_VMEM,
        cost_estimate=cost(2**27, 2**21),
    )(x, u, y, d)


def hidden_kernel(at, r, w2, w3, out, p0, p1, p2, p3, cut):
    w2 = w2[0]
    w3 = w3[0]
    g2 = g3 = None
    for s in range(NS):
        v = r[s * NG : (s + 1) * NG].astype(F32)
        fm = v[:, :NB].reshape(TILE, T).astype(BF)
        bd = v[:, NB:].reshape(TILE, T).astype(BF)
        pre = mm(w2, fm, TN) * S1
        dgated = mm(w3, bd, NN) * S5
        th = jnp.tanh(C0 * (pre + 0.044715 * (pre * pre * pre)))
        cdf = 0.5 * (1.0 + th)
        gated = (pre * cdf).astype(BF)
        slope = cdf + (0.5 * C0) * pre * (1.0 - th * th) * (1.0 + (3 * 0.044715) * (pre * pre))
        dpre = (dgated * slope).astype(BF)
        down = mm(w3, gated, TN) * S5
        back_up = mm(w2, dpre, NN) * S1
        a2 = mm(fm, dpre, NT)
        a3 = mm(gated, bd, NT)
        g2, g3 = (a2, a3) if g2 is None else (g2 + a2, g3 + a3)
        both = jnp.concatenate([down.reshape(NG, NB, T), back_up.reshape(NG, NB, T)], 1)
        out[s * NG : (s + 1) * NG] = both.astype(BF)
    for c in range(4):
        v = (g2[:, c * 128 : (c + 1) * 128] * S1).reshape(NZ, NS, R, 128)
        for s in range(NS):
            cut[:, s, c * R : (c + 1) * R] = v[:, s]
    cut[:, :, 4 * R :] = (g3 * S5).reshape(NZ, NS, 4 * R, 128)
    for k, p in enumerate((p0, p1, p2, p3)):
        for h in range(2):
            p[h * NS : (h + 1) * NS] = cut[(at[0] ^ k) * 2 + h].astype(BF)


def hidden_stage(at, r, up2, dn1):
    spec = pltpu.PrefetchScalarGridSpec(
        num_scalar_prefetch=1,
        grid=(ML,),
        in_specs=[
            pl.BlockSpec((NS * NG, 2 * NB, T), lambda m, s: (0, m, 0)),
            pl.BlockSpec((1, TILE, HB), lambda m, s: (s[2] * ML + m, 0, 0)),
            pl.BlockSpec((1, HB, TILE), lambda m, s: (s[2] * ML + m, 0, 0)),
        ],
        out_specs=[pl.BlockSpec((NS * NG, 2 * NB, T), lambda m, s: (0, m, 0))]
        + [pl.BlockSpec((2 * NS, 8 * R, 128), lambda m, s: (0, m, 0))] * NQ,
        scratch_shapes=[pltpu.VMEM((NZ, NS, 8 * R, 128), F32)],
    )
    return pl.pallas_call(
        hidden_kernel,
        grid_spec=spec,
        out_shape=[pltpu.HBM((NS * NG, 2 * NB * ML, T), BF)]
        + [pltpu.HBM((2 * NS, 8 * R * ML, 128), BF)] * NQ,
        compiler_params=PARAMS,
        cost_estimate=cost(2**30, 2**22),
    )(at, r, up2, dn1)


def outer_kernel(r, x, y, u, p0, p1, p2, p3, gin, grads, rows, cut, held, sems):
    copies = [pltpu.make_async_copy(p, held.at[k], sems.at[k]) for k, p in enumerate((p0, p1, p2, p3))]
    for copy in copies:
        copy.start()
    for s in range(NS):
        for h in range(2):
            rows[h, :, s] = r[s * NG : (s + 1) * NG, :, h * 128 : (h + 1) * 128].astype(F32)
    flat = rows.reshape(2, TILE * 2 * NB, 128)

    def pick(j):
        return jnp.concatenate([flat[h, pl.ds(j, TILE, stride=2 * NB), :] for h in range(2)], 1).astype(BF)

    for b in range(NB):
        f = slice(b * TILE, (b + 1) * TILE)
        down, back_up = pick(b), pick(NB + b)
        gin[:, f] = (mm(back_up, u[b], TT) * S1).astype(BF)
        g1 = (mm(x[:, f], back_up, TT) * S1).reshape(NZ, NS, R, TILE)
        g4 = (mm(down, y[:, f], NN) * S1).reshape(NZ, NS, R, TILE)
        for s in range(NS):
            cut[s, :, b * R : (b + 1) * R] = g1[:, s]
            cut[s, :, (NB + b) * R : (NB + b + 1) * R] = g4[:, s]
    grads[:, :NZ] = cut[...].astype(BF)
    for copy in copies:
        copy.wait()
    g23 = (held[0].astype(F32) + held[1].astype(F32)) + (held[2].astype(F32) + held[3].astype(F32))
    g23 = g23.astype(BF)
    for h in range(2):
        grads[:, NZ + h] = g23[h * NS : (h + 1) * NS]


def outer_stage(r, x, y, u, p):
    return pl.pallas_call(
        outer_kernel,
        in_specs=[pl.BlockSpec(memory_space=pltpu.VMEM)] * 4 + [pl.BlockSpec(memory_space=pltpu.HBM)] * NQ,
        out_shape=[
            jax.ShapeDtypeStruct((T, NB * TILE), BF),
            jax.ShapeDtypeStruct((NS, NZ + 2, 2 * NB * R, TILE), BF),
        ],
        scratch_shapes=[
            pltpu.VMEM((2, NG, NS, 2 * NB * ML, 128), F32),
            pltpu.VMEM((NS, NZ, 2 * NB * R, TILE), F32),
            pltpu.VMEM((NQ, 2 * NS, 8 * R * ML, 128), BF),
            pltpu.SemaphoreType.DMA((NQ,)),
        ],
        compiler_params=FULL,
        cost_estimate=cost(2**10, 2**10),
    )(r, x, y, u, *p)


def near_kernel(at, a, g14, keep, give):
    v = a[0, :NZ].astype(F32)
    for s in range(1, NS):
        v = v + a[s, :NZ].astype(F32)
    g14[...] = v.astype(BF)
    keep[...] = a[:, NZ + at[1]]
    give[...] = a[:, NZ + 1 - at[1]]


def near_stage(at, a):
    return pl.pallas_call(
        near_kernel,
        in_specs=[pl.BlockSpec(memory_space=pltpu.SMEM), pl.BlockSpec(memory_space=pltpu.VMEM)],
        out_shape=[
            jax.ShapeDtypeStruct((NZ, 2 * NB * R, TILE), BF),
            jax.ShapeDtypeStruct((NS, 8 * R * ML, 128), BF),
            jax.ShapeDtypeStruct((NS, 8 * R * ML, 128), BF),
        ],
        compiler_params=PARAMS,
        cost_estimate=cost(2**10, 2**10),
    )(at, a)


def choose(sub, options):
    v = options[-1]
    for s in range(len(options) - 2, -1, -1):
        v = jnp.where(sub == s, options[s], v)
    return v


def step(weight, grad, dither):
    noise = GRID * (dither.astype(F32) / 32768.0 - 0.5)
    return (weight - RATE * grad + noise).astype(BF)


def own_rows(sub, block):
    v = block.astype(F32)
    return choose(sub, [v[:, s * R : (s + 1) * R] for s in range(NS)])


def update_kernel(at, a, keep, took, up1, up2, dn1, dn2, d1, d2, d3, d4, n1, n2, n3, n4):
    sub = at[2]
    v = a[0].astype(F32)
    for z in range(1, NZ):
        v = v + a[z].astype(F32)
    g = v.reshape(2, NB, R, TILE)
    n1[...] = step(own_rows(sub, up1[...]), g[0], d1[...])
    n4[...] = step(own_rows(sub, dn2[...]), g[1], d4[...])
    own = own_rows(sub, up2[...])
    for s in range(NS):
        v = keep[s].astype(F32) + took[s].astype(F32)
        for i in range(ML):
            m = s * ML + i
            w = v[i * 8 * R : (i + 1) * 8 * R]
            grad = jnp.concatenate([w[c * R : (c + 1) * R] for c in range(4)], 1)
            n2[m] = step(own[m], grad, d2[m])
            n3[m] = step(dn1[m].astype(F32), w[4 * R :], d3[m])


def update(at, a, keep, took, up1, up2, dn1, dn2, d1, d2, d3, d4):
    def whole(*shape):
        return pl.BlockSpec(shape, lambda i, s: (0,) * len(shape))

    def far(s):
        return s[0] * 2 + s[1]

    small = whole(NB, R, TILE)
    wide = whole(NB, R, HB)
    large = whole(NB, 4 * R, TILE)
    half = whole(NS, 8 * R * ML, 128)
    block = pl.BlockSpec((NB, NS * R, TILE), lambda i, s: (0, far(s), 0))
    spec = pltpu.PrefetchScalarGridSpec(
        num_scalar_prefetch=1,
        grid=(1,),
        in_specs=[
            whole(NZ, 2 * NB * R, TILE),
            half,
            half,
            block,
            pl.BlockSpec((NB, NS * R, HB), lambda i, s: (0, far(s), 0)),
            pl.BlockSpec((NB, 4 * R, TILE), lambda i, s: (0, far(s) * NS + s[2], 0)),
            block,
            small,
            wide,
            large,
            small,
        ],
        out_specs=[small, wide, large, small],
    )
    shapes = ((NB, R, TILE), (NB, R, HB), (NB, 4 * R, TILE), (NB, R, TILE))
    return pl.pallas_call(
        update_kernel,
        grid_spec=spec,
        out_shape=[jax.ShapeDtypeStruct(shape, BF) for shape in shapes],
        compiler_params=PARAMS,
        cost_estimate=cost(2**10, 2**10),
    )(at, a, keep, took, up1, up2, dn1, dn2, d1, d2, d3, d4)


def on_device(x, dy, up1, up2, dn1, dn2, di1, di2, di3, di4):
    at = jnp.stack([lax.axis_index(a) for a in ("fq", "z1", SUB)]).astype(jnp.int32)
    got = exchange(first_stage(x, up1, dy, dn2), GROUP)
    send, *p = hidden_stage(at, got, up2, dn1)
    p = [p[0]] + [lax.ppermute(p[k], "fq", [(i, i ^ k) for i in range(NQ)]) for k in range(1, NQ)]
    gin, grads = outer_stage(exchange(send, GROUP), x, dy, up1, p)
    g14, keep, give = near_stage(at, exchange(grads, SUB))
    took = lax.ppermute(give, "z1", [(0, 1), (1, 0)])
    new1, new2, new3, new4 = update(at, exchange(g14, FAR), keep, took, up1, up2, dn1, dn2, di1, di2, di3, di4)
    return gin, new1, new2, new3, new4


def solution(mesh):
    dp, mp = mesh.shape["dp"], mesh.shape["mp"]
    fine = Mesh(mesh.devices.reshape(dp // 8, 2, 2, 2, mp), ("fq", "z1", "zl", "yl", "mp"))
    w = P("mp", None, None)
    d = P("mp", DP, None)
    return jax.shard_map(
        on_device,
        mesh=fine,
        in_specs=(P(DP, "mp"), P(DP, "mp"), w, w, w, w, d, d, d, d),
        out_specs=(P(DP, "mp"), d, d, d, d),
        check_vma=False,
    )
```

```python
import math

import jax
import jax.numpy as jnp
from jax import lax
from jax.experimental import pallas as pl
from jax.experimental.pallas import tpu as pltpu
from jax.sharding import Mesh, PartitionSpec as P

TILE = 128
HB = 512
T = 256
NB = 8
NS = 4
NG = 16
NZ = 8
NQ = 4
ML = NB // NS
R = TILE // (NZ * NS)
GRID = 0.25
RATE = 4.0 / math.sqrt(8192)
S1 = TILE ** -0.5
S5 = HB ** -0.5
C0 = math.sqrt(2.0 / math.pi)
BF = jnp.bfloat16
F32 = jnp.float32

DP = ("fq", "z1", "zl", "yl")
SUB = ("zl", "yl")
NEAR = ("z1", "zl", "yl")
FAR = ("fq",)
GROUP = SUB + ("mp",)

NN = (((1,), (0,)), ((), ()))
NT = (((1,), (1,)), ((), ()))
TN = (((0,), (0,)), ((), ()))
TT = (((0,), (1,)), ((), ()))
PARAMS = pltpu.CompilerParams(vmem_limit_bytes=48 << 20)
FULL = pltpu.CompilerParams(vmem_limit_bytes=64 << 20)
ALL_VMEM = pltpu.CompilerParams(vmem_limit_bytes=60 << 20)


def mm(a, b, dims):
    return lax.dot_general(a, b, dims, preferred_element_type=F32)


def exchange(a, axes):
    return lax.all_to_all(a, axes, 0, 0, tiled=True)


def cost(flops, moved):
    return pl.CostEstimate(flops=flops, bytes_accessed=moved, transcendentals=0)


def first_kernel(x, u, y, d, out, rows):
    for h in range(2):
        t = slice(h * 128, (h + 1) * 128)
        for b in range(NB):
            f = slice(b * TILE, (b + 1) * TILE)
            rows[h, pl.ds(b, TILE, stride=2 * NB), :] = mm(u[b], x[t, f], TT) * S1
            rows[h, pl.ds(NB + b, TILE, stride=2 * NB), :] = mm(d[b], y[t, f], NT) * S1
    for h in range(2):
        v = rows[h].reshape(NG, NS, 2 * NB * ML, 128).astype(BF)
        for s in range(NS):
            out[s * NG : (s + 1) * NG, :, h * 128 : (h + 1) * 128] = v[:, s]


def first_stage(x, u, y, d):
    return pl.pallas_call(
        first_kernel,
        out_shape=jax.ShapeDtypeStruct((NS * NG, 2 * NB * ML, T), BF),
        scratch_shapes=[pltpu.VMEM((2, TILE * 2 * NB, 128), F32)],
        compiler_params=ALL_VMEM,
        cost_estimate=cost(2**27, 2**21),
    )(x, u, y, d)


def hidden_kernel(at, r, w2, w3, out, g, cut):
    w2 = w2[0]
    w3 = w3[0]
    g2 = g3 = None
    for s in range(NS):
        v = r[s * NG : (s + 1) * NG].astype(F32)
        fm = v[:, :NB].reshape(TILE, T).astype(BF)
        bd = v[:, NB:].reshape(TILE, T).astype(BF)
        pre = mm(w2, fm, TN) * S1
        dgated = mm(w3, bd, NN) * S5
        th = jnp.tanh(C0 * (pre + 0.044715 * (pre * pre * pre)))
        cdf = 0.5 * (1.0 + th)
        gated = (pre * cdf).astype(BF)
        slope = cdf + (0.5 * C0) * pre * (1.0 - th * th) * (1.0 + (3 * 0.044715) * (pre * pre))
        dpre = (dgated * slope).astype(BF)
        down = mm(w3, gated, TN) * S5
        back_up = mm(w2, dpre, NN) * S1
        a2 = mm(fm, dpre, NT)
        a3 = mm(gated, bd, NT)
        g2, g3 = (a2, a3) if g2 is None else (g2 + a2, g3 + a3)
        both = jnp.concatenate([down.reshape(NG, NB, T), back_up.reshape(NG, NB, T)], 1)
        out[s * NG : (s + 1) * NG] = both.astype(BF)
    for c in range(4):
        v = (g2[:, c * 128 : (c + 1) * 128] * S1).reshape(NZ, NS, R, 128)
        for s in range(NS):
            cut[:, s, c * R : (c + 1) * R] = v[:, s]
    cut[:, :, 4 * R :] = (g3 * S5).reshape(NZ, NS, 4 * R, 128)
    for z in range(NZ):
        g[(z % 2) * NS : (z % 2 + 1) * NS, z // 2] = cut[z].astype(BF)


def hidden_stage(at, r, up2, dn1):
    spec = pltpu.PrefetchScalarGridSpec(
        num_scalar_prefetch=1,
        grid=(ML,),
        in_specs=[
            pl.BlockSpec((NS * NG, 2 * NB, T), lambda m, s: (0, m, 0)),
            pl.BlockSpec((1, TILE, HB), lambda m, s: (s[2] * ML + m, 0, 0)),
            pl.BlockSpec((1, HB, TILE), lambda m, s: (s[2] * ML + m, 0, 0)),
        ],
        out_specs=[pl.BlockSpec((NS * NG, 2 * NB, T), lambda m, s: (0, m, 0))]
        + [pl.BlockSpec((2 * NS, NQ, 8 * R, 128), lambda m, s: (0, 0, m, 0))],
        scratch_shapes=[pltpu.VMEM((NZ, NS, 8 * R, 128), F32)],
    )
    return pl.pallas_call(
        hidden_kernel,
        grid_spec=spec,
        out_shape=[pltpu.HBM((NS * NG, 2 * NB * ML, T), BF)]
        + [pltpu.HBM((2 * NS, NQ, 8 * R * ML, 128), BF)],
        compiler_params=PARAMS,
        cost_estimate=cost(2**30, 2**22),
    )(at, r, up2, dn1)


def outer_kernel(r, x, y, u, g23, gin, grads, rows, cut, sem):
    copy = pltpu.make_async_copy(g23, grads.at[:, :, 1], sem)
    copy.start()
    for s in range(NS):
        for h in range(2):
            rows[h, :, s] = r[s * NG : (s + 1) * NG, :, h * 128 : (h + 1) * 128].astype(F32)
    flat = rows.reshape(2, TILE * 2 * NB, 128)

    def pick(j):
        return jnp.concatenate([flat[h, pl.ds(j, TILE, stride=2 * NB), :] for h in range(2)], 1).astype(BF)

    for b in range(NB):
        f = slice(b * TILE, (b + 1) * TILE)
        down, back_up = pick(b), pick(NB + b)
        gin[:, f] = (mm(back_up, u[b], TT) * S1).astype(BF)
        g1 = (mm(x[:, f], back_up, TT) * S1).reshape(NZ, NS, R, TILE)
        g4 = (mm(down, y[:, f], NN) * S1).reshape(NZ, NS, R, TILE)
        for s in range(NS):
            cut[:, s, b * R : (b + 1) * R] = g1[:, s]
            cut[:, s, (NB + b) * R : (NB + b + 1) * R] = g4[:, s]
    for z in range(NZ):
        grads[(z % 2) * NS : (z % 2 + 1) * NS, z // 2, 0] = cut[z].astype(BF)
    copy.wait()


def outer_stage(r, x, y, u, g23):
    return pl.pallas_call(
        outer_kernel,
        in_specs=[pl.BlockSpec(memory_space=pltpu.VMEM)] * 4 + [pl.BlockSpec(memory_space=pltpu.HBM)],
        out_shape=[
            jax.ShapeDtypeStruct((T, NB * TILE), BF),
            jax.ShapeDtypeStruct((2 * NS, NQ, 2, 2 * NB * R, TILE), BF),
        ],
        scratch_shapes=[
            pltpu.VMEM((2, NG, NS, 2 * NB * ML, 128), F32),
            pltpu.VMEM((NZ, NS, 2 * NB * R, TILE), F32),
            pltpu.SemaphoreType.DMA,
        ],
        compiler_params=PARAMS,
        cost_estimate=cost(2**10, 2**10),
    )(r, x, y, u, g23)


def near_kernel(a, out):
    for q in range(NQ):
        v = a[0, q, 0].astype(F32)
        for n in range(1, 2 * NS):
            v = v + a[n, q, 0].astype(F32)
        out[q, 0] = v.astype(BF)
        for s in range(NS):
            out[q, 1 + s] = (a[s, q, 1].astype(F32) + a[NS + s, q, 1].astype(F32)).astype(BF)


def near_stage(a):
    return pl.pallas_call(
        near_kernel,
        out_shape=jax.ShapeDtypeStruct((NQ, 1 + NS, 2 * NB * R, TILE), BF),
        compiler_params=PARAMS,
        cost_estimate=cost(2**10, 2**10),
    )(a)


def choose(sub, options):
    v = options[-1]
    for s in range(len(options) - 2, -1, -1):
        v = jnp.where(sub == s, options[s], v)
    return v


def step(weight, grad, dither):
    noise = GRID * (dither.astype(F32) / 32768.0 - 0.5)
    return (weight - RATE * grad + noise).astype(BF)


def own_rows(sub, block):
    v = block.astype(F32)
    return choose(sub, [v[:, s * R : (s + 1) * R] for s in range(NS)])


def update_kernel(at, a, up1, up2, dn1, dn2, d1, d2, d3, d4, n1, n2, n3, n4):
    sub = at[2]

    def total(i):
        return (a[0, i].astype(F32) + a[1, i].astype(F32)) + (a[2, i].astype(F32) + a[3, i].astype(F32))

    g = total(0).reshape(2, NB, R, TILE)
    n1[...] = step(own_rows(sub, up1[...]), g[0], d1[...])
    n4[...] = step(own_rows(sub, dn2[...]), g[1], d4[...])
    own = own_rows(sub, up2[...])
    for s in range(NS):
        v = total(1 + s)
        for i in range(ML):
            m = s * ML + i
            w = v[i * 8 * R : (i + 1) * 8 * R]
            grad = jnp.concatenate([w[c * R : (c + 1) * R] for c in range(4)], 1)
            n2[m] = step(own[m], grad, d2[m])
            n3[m] = step(dn1[m].astype(F32), w[4 * R :], d3[m])


def update(at, a, up1, up2, dn1, dn2, d1, d2, d3, d4):
    def whole(*shape):
        return pl.BlockSpec(shape, lambda i, s: (0,) * len(shape))

    def far(s):
        return s[0] * 2 + s[1]

    small = whole(NB, R, TILE)
    wide = whole(NB, R, HB)
    large = whole(NB, 4 * R, TILE)
    block = pl.BlockSpec((NB, NS * R, TILE), lambda i, s: (0, far(s), 0))
    spec = pltpu.PrefetchScalarGridSpec(
        num_scalar_prefetch=1,
        grid=(1,),
        in_specs=[
            whole(NQ, 1 + NS, 2 * NB * R, TILE),
            block,
            pl.BlockSpec((NB, NS * R, HB), lambda i, s: (0, far(s), 0)),
            pl.BlockSpec((NB, 4 * R, TILE), lambda i, s: (0, far(s) * NS + s[2], 0)),
            block,
            small,
            wide,
            large,
            small,
        ],
        out_specs=[small, wide, large, small],
    )
    shapes = ((NB, R, TILE), (NB, R, HB), (NB, 4 * R, TILE), (NB, R, TILE))
    return pl.pallas_call(
        update_kernel,
        grid_spec=spec,
        out_shape=[jax.ShapeDtypeStruct(shape, BF) for shape in shapes],
        compiler_params=PARAMS,
        cost_estimate=cost(2**10, 2**10),
    )(at, a, up1, up2, dn1, dn2, d1, d2, d3, d4)


def on_device(x, dy, up1, up2, dn1, dn2, di1, di2, di3, di4):
    at = jnp.stack([lax.axis_index(a) for a in ("fq", "z1", SUB)]).astype(jnp.int32)
    got = exchange(first_stage(x, up1, dy, dn2), GROUP)
    send, g23 = hidden_stage(at, got, up2, dn1)
    gin, grads = outer_stage(exchange(send, GROUP), x, dy, up1, g23)
    grads = exchange(near_stage(exchange(grads, NEAR)), FAR)
    new1, new2, new3, new4 = update(at, grads, up1, up2, dn1, dn2, di1, di2, di3, di4)
    return gin, new1, new2, new3, new4


def solution(mesh):
    dp, mp = mesh.shape["dp"], mesh.shape["mp"]
    fine = Mesh(mesh.devices.reshape(dp // 8, 2, 2, 2, mp), ("fq", "z1", "zl", "yl", "mp"))
    w = P("mp", None, None)
    d = P("mp", DP, None)
    return jax.shard_map(
        on_device,
        mesh=fine,
        in_specs=(P(DP, "mp"), P(DP, "mp"), w, w, w, w, d, d, d, d),
        out_specs=(P(DP, "mp"), d, d, d, d),
        check_vma=False,
    )
```

```python
import math

import jax
import jax.numpy as jnp
from jax import lax
from jax.experimental import pallas as pl
from jax.experimental.pallas import tpu as pltpu
from jax.sharding import Mesh, PartitionSpec as P

TILE = 128
HB = 512
T = 256
NB = 8
NS = 4
NG = 16
NZ = 8
ML = NB // NS
R = TILE // (NZ * NS)
GRID = 0.25
RATE = 4.0 / math.sqrt(8192)
S1 = TILE ** -0.5
S5 = HB ** -0.5
C0 = math.sqrt(2.0 / math.pi)
BF = jnp.bfloat16
F32 = jnp.float32

DP = ("zh", "zl", "yl")
SUB = ("zl", "yl")
FAR = ("zh",)
GROUP = SUB + ("mp",)

NN = (((1,), (0,)), ((), ()))
NT = (((1,), (1,)), ((), ()))
TN = (((0,), (0,)), ((), ()))
TT = (((0,), (1,)), ((), ()))
PARAMS = pltpu.CompilerParams(vmem_limit_bytes=48 << 20)
ALL_VMEM = pltpu.CompilerParams(vmem_limit_bytes=60 << 20)


def mm(a, b, dims):
    return lax.dot_general(a, b, dims, preferred_element_type=F32)


def exchange(a, axes):
    return lax.all_to_all(a, axes, 0, 0, tiled=True)


def cost(flops, moved):
    return pl.CostEstimate(flops=flops, bytes_accessed=moved, transcendentals=0)


def first_kernel(x, u, y, d, out, rows):
    for h in range(2):
        t = slice(h * 128, (h + 1) * 128)
        for b in range(NB):
            f = slice(b * TILE, (b + 1) * TILE)
            rows[h, pl.ds(b, TILE, stride=2 * NB), :] = mm(u[b], x[t, f], TT) * S1
            rows[h, pl.ds(NB + b, TILE, stride=2 * NB), :] = mm(d[b], y[t, f], NT) * S1
    for h in range(2):
        v = rows[h].reshape(NG, NS, 2 * NB * ML, 128).astype(BF)
        for s in range(NS):
            out[s * NG : (s + 1) * NG, :, h * 128 : (h + 1) * 128] = v[:, s]


def first_stage(x, u, y, d):
    return pl.pallas_call(
        first_kernel,
        out_shape=jax.ShapeDtypeStruct((NS * NG, 2 * NB * ML, T), BF),
        scratch_shapes=[pltpu.VMEM((2, TILE * 2 * NB, 128), F32)],
        compiler_params=ALL_VMEM,
        cost_estimate=cost(2**27, 2**21),
    )(x, u, y, d)


def hidden_kernel(sub, r, w2, w3, out, g):
    w2 = w2[0]
    w3 = w3[0]
    g2 = g3 = None
    for s in range(NS):
        v = r[s * NG : (s + 1) * NG].astype(F32)
        fm = v[:, :NB].reshape(TILE, T).astype(BF)
        bd = v[:, NB:].reshape(TILE, T).astype(BF)
        pre = mm(w2, fm, TN) * S1
        dgated = mm(w3, bd, NN) * S5
        th = jnp.tanh(C0 * (pre + 0.044715 * (pre * pre * pre)))
        cdf = 0.5 * (1.0 + th)
        gated = (pre * cdf).astype(BF)
        slope = cdf + (0.5 * C0) * pre * (1.0 - th * th) * (1.0 + (3 * 0.044715) * (pre * pre))
        dpre = (dgated * slope).astype(BF)
        down = mm(w3, gated, TN) * S5
        back_up = mm(w2, dpre, NN) * S1
        a2 = mm(fm, dpre, NT)
        a3 = mm(gated, bd, NT)
        g2, g3 = (a2, a3) if g2 is None else (g2 + a2, g3 + a3)
        both = jnp.concatenate([down.reshape(NG, NB, T), back_up.reshape(NG, NB, T)], 1)
        out[s * NG : (s + 1) * NG] = both.astype(BF)
    g2 = (g2 * S1).astype(BF)
    g3 = (g3 * S5).astype(BF)
    for c in range(4):
        g[:, c * 16 : (c + 1) * 16] = g2[:, c * 128 : (c + 1) * 128].reshape(NZ, 16, 128)
    g[:, 64:] = g3.reshape(NZ, 64, 128)


def hidden_stage(sub, r, up2, dn1):
    spec = pltpu.PrefetchScalarGridSpec(
        num_scalar_prefetch=1,
        grid=(ML,),
        in_specs=[
            pl.BlockSpec((NS * NG, 2 * NB, T), lambda m, s: (0, m, 0)),
            pl.BlockSpec((1, TILE, HB), lambda m, s: (s[0] * ML + m, 0, 0)),
            pl.BlockSpec((1, HB, TILE), lambda m, s: (s[0] * ML + m, 0, 0)),
        ],
        out_specs=[
            pl.BlockSpec((NS * NG, 2 * NB, T), lambda m, s: (0, m, 0)),
            pl.BlockSpec((NZ, 128, 128), lambda m, s: (0, m, 0)),
        ],
    )
    return pl.pallas_call(
        hidden_kernel,
        grid_spec=spec,
        out_shape=[
            pltpu.HBM((NS * NG, 2 * NB * ML, T), BF),
            pltpu.HBM((NZ, 128 * ML, 128), BF),
        ],
        compiler_params=PARAMS,
        cost_estimate=cost(2**30, 2**22),
    )(sub, r, up2, dn1)


def outer_kernel(r, x, y, u, gin, g14, rows, cut):
    for s in range(NS):
        for h in range(2):
            rows[h, :, s] = r[s * NG : (s + 1) * NG, :, h * 128 : (h + 1) * 128].astype(F32)
    flat = rows.reshape(2, TILE * 2 * NB, 128)

    def pick(j):
        return jnp.concatenate([flat[h, pl.ds(j, TILE, stride=2 * NB), :] for h in range(2)], 1).astype(BF)

    for b in range(NB):
        f = slice(b * TILE, (b + 1) * TILE)
        down, back_up = pick(b), pick(NB + b)
        gin[:, f] = (mm(back_up, u[b], TT) * S1).astype(BF)
        g1 = (mm(x[:, f], back_up, TT) * S1).reshape(NZ, NS, R, TILE)
        g4 = (mm(down, y[:, f], NN) * S1).reshape(NZ, NS, R, TILE)
        for s in range(NS):
            cut[s, :, b * R : (b + 1) * R] = g1[:, s]
            cut[s, :, (NB + b) * R : (NB + b + 1) * R] = g4[:, s]
    g14[...] = cut[...].astype(BF)


def outer_stage(r, x, y, u):
    return pl.pallas_call(
        outer_kernel,
        out_shape=[
            jax.ShapeDtypeStruct((T, NB * TILE), BF),
            jax.ShapeDtypeStruct((NS, NZ, 2 * NB * R, TILE), BF),
        ],
        scratch_shapes=[
            pltpu.VMEM((2, NG, NS, 2 * NB * ML, 128), F32),
            pltpu.VMEM((NS, NZ, 2 * NB * R, TILE), F32),
        ],
        compiler_params=PARAMS,
        cost_estimate=cost(2**27, 2**21),
    )(r, x, y, u)


def near_sum_kernel(a, out):
    v = a[0].astype(F32)
    for s in range(1, NS):
        v = v + a[s].astype(F32)
    out[...] = v.astype(BF)


def near_sum(a):
    return pl.pallas_call(
        near_sum_kernel, out_shape=jax.ShapeDtypeStruct(a.shape[1:], BF), cost_estimate=cost(2**10, 2**10)
    )(a)


def choose(sub, options):
    v = options[-1]
    for s in range(len(options) - 2, -1, -1):
        v = jnp.where(sub == s, options[s], v)
    return v


def split_kernel(r, out):
    v = r[...].astype(F32)
    for s in range(NS):
        parts = []
        for m in range(ML):
            w = v[m * 128 : (m + 1) * 128]
            parts += [w[c * 16 + s * R : c * 16 + (s + 1) * R] for c in range(4)]
            parts.append(w[64 + s * 16 : 64 + (s + 1) * 16])
        out[s] = jnp.concatenate(parts, 0).astype(BF)


def split_rows(r):
    return pl.pallas_call(
        split_kernel,
        out_shape=jax.ShapeDtypeStruct((NS, 32 * ML, 128), BF),
        cost_estimate=cost(2**10, 2**10),
    )(r)


def step(weight, grad, dither):
    noise = GRID * (dither.astype(F32) / 32768.0 - 0.5)
    return (weight - RATE * grad + noise).astype(BF)


def own_rows(sub, block):
    v = block.astype(F32)
    return choose(sub, [v[:, s * R : (s + 1) * R] for s in range(NS)])


def update_kernel(at, a, q, up1, up2, dn1, dn2, d1, d2, d3, d4, n1, n2, n3, n4):
    sub = at[1]
    v = a[0].astype(F32)
    for z in range(1, NZ):
        v = v + a[z].astype(F32)
    g = v.reshape(2, NB, R, TILE)
    n1[...] = step(own_rows(sub, up1[...]), g[0], d1[...])
    n4[...] = step(own_rows(sub, dn2[...]), g[1], d4[...])
    own = own_rows(sub, up2[...])
    for s in range(NS):
        v = q[s].astype(F32)
        for i in range(ML):
            m = s * ML + i
            w = v[i * 8 * R : (i + 1) * 8 * R]
            grad = jnp.concatenate([w[c * R : (c + 1) * R] for c in range(4)], 1)
            n2[m] = step(own[m], grad, d2[m])
            n3[m] = step(dn1[m].astype(F32), w[4 * R :], d3[m])


def update(at, a, q, up1, up2, dn1, dn2, d1, d2, d3, d4):
    def whole(*shape):
        return pl.BlockSpec(shape, lambda i, s: (0,) * len(shape))

    def far(s):
        return s[0]

    small = whole(NB, R, TILE)
    wide = whole(NB, R, HB)
    large = whole(NB, 4 * R, TILE)
    block = pl.BlockSpec((NB, NS * R, TILE), lambda i, s: (0, far(s), 0))
    spec = pltpu.PrefetchScalarGridSpec(
        num_scalar_prefetch=1,
        grid=(1,),
        in_specs=[
            whole(NZ, 2 * NB * R, TILE),
            whole(NS, 8 * R * ML, 128),
            block,
            pl.BlockSpec((NB, NS * R, HB), lambda i, s: (0, far(s), 0)),
            pl.BlockSpec((NB, 4 * R, TILE), lambda i, s: (0, far(s) * NS + s[1], 0)),
            block,
            small,
            wide,
            large,
            small,
        ],
        out_specs=[small, wide, large, small],
    )
    shapes = ((NB, R, TILE), (NB, R, HB), (NB, 4 * R, TILE), (NB, R, TILE))
    return pl.pallas_call(
        update_kernel,
        grid_spec=spec,
        out_shape=[jax.ShapeDtypeStruct(shape, BF) for shape in shapes],
        compiler_params=PARAMS,
        cost_estimate=cost(2**10, 2**10),
    )(at, a, q, up1, up2, dn1, dn2, d1, d2, d3, d4)


def on_device(x, dy, up1, up2, dn1, dn2, di1, di2, di3, di4):
    sub = lax.axis_index(SUB).astype(jnp.int32)
    far = lax.axis_index(FAR).astype(jnp.int32)
    at = jnp.stack([far, sub])
    sub1 = sub.reshape(1)

    got = exchange(first_stage(x, up1, dy, dn2), GROUP)
    send, g23 = hidden_stage(sub1, got, up2, dn1)
    r23 = lax.psum_scatter(g23, FAR, scatter_dimension=0, tiled=True).reshape(128 * ML, 128)

    def tail(send, x, dy, up1):
        gin, g14 = outer_stage(exchange(send, GROUP), x, dy, up1)
        return gin, exchange(near_sum(exchange(g14, SUB)), FAR)

    def never(send, x, dy, up1):
        return jnp.zeros((T, NB * TILE), BF), jnp.zeros((NZ, 2 * NB * R, TILE), BF)

    gin, g14 = lax.cond(lax.axis_index("mp") < 999, tail, never, send, x, dy, up1)
    g14, r23, gin = lax.optimization_barrier((g14, r23, gin))
    q = exchange(split_rows(r23), SUB)
    new1, new2, new3, new4 = update(at, g14, q, up1, up2, dn1, dn2, di1, di2, di3, di4)
    return gin, new1, new2, new3, new4


def solution(mesh):
    dp, mp = mesh.shape["dp"], mesh.shape["mp"]
    fine = Mesh(mesh.devices.reshape(dp // 4, 2, 2, mp), ("zh", "zl", "yl", "mp"))
    w = P("mp", None, None)
    d = P("mp", DP, None)
    return jax.shard_map(
        on_device,
        mesh=fine,
        in_specs=(P(DP, "mp"), P(DP, "mp"), w, w, w, w, d, d, d, d),
        out_specs=(P(DP, "mp"), d, d, d, d),
        check_vma=False,
    )
```

```python
import math

import jax
import jax.numpy as jnp
from jax import lax
from jax.experimental import pallas as pl
from jax.experimental.pallas import tpu as pltpu
from jax.sharding import Mesh, PartitionSpec as P

TILE = 128
HB = 512
T = 256
NB = 8
NS = 4
NG = 16
NZ = 8
NQ = 4
ML = NB // NS
R = TILE // (NZ * NS)
GRID = 0.25
RATE = 4.0 / math.sqrt(8192)
S1 = TILE ** -0.5
S5 = HB ** -0.5
C0 = math.sqrt(2.0 / math.pi)
BF = jnp.bfloat16
F32 = jnp.float32

DP = ("fq", "z1", "zl", "yl")
SUB = ("zl", "yl")
NEAR = ("z1", "zl", "yl")
FAR = ("fq",)
GROUP = SUB + ("mp",)

NN = (((1,), (0,)), ((), ()))
NT = (((1,), (1,)), ((), ()))
TN = (((0,), (0,)), ((), ()))
TT = (((0,), (1,)), ((), ()))
PARAMS = pltpu.CompilerParams(vmem_limit_bytes=48 << 20)
FULL = pltpu.CompilerParams(vmem_limit_bytes=64 << 20)


def mm(a, b, dims):
    return lax.dot_general(a, b, dims, preferred_element_type=F32)


def exchange(a, axes):
    return lax.all_to_all(a, axes, 0, 0, tiled=True)


def cost(flops, moved):
    return pl.CostEstimate(flops=flops, bytes_accessed=moved, transcendentals=0)


def first_kernel(x_in, u_in, y_in, d_in, out, x, u, y, d, rows, sent, sems):
    pairs = ((x_in, x), (u_in, u), (y_in, y), (d_in, d))
    loads = [pltpu.make_async_copy(a, b, sems.at[i]) for i, (a, b) in enumerate(pairs)]
    for load in loads:
        load.start()
    loads[0].wait()
    loads[1].wait()
    for h in range(2):
        t = slice(h * 128, (h + 1) * 128)
        for b in range(NB):
            f = slice(b * TILE, (b + 1) * TILE)
            rows[h, pl.ds(b, TILE, stride=2 * NB), :] = mm(u[b], x[t, f], TT) * S1
    loads[2].wait()
    loads[3].wait()
    for h in range(2):
        t = slice(h * 128, (h + 1) * 128)
        for b in range(NB):
            f = slice(b * TILE, (b + 1) * TILE)
            rows[h, pl.ds(NB + b, TILE, stride=2 * NB), :] = mm(d[b], y[t, f], NT) * S1
    view = rows.reshape(2, NG, NS, 2 * NB * ML, 128)
    stores = []
    for s in range(NS):
        for h in range(2):
            sent[s, :, :, h * 128 : (h + 1) * 128] = view[h, :, s].astype(BF)
        store = pltpu.make_async_copy(sent.at[s], out.at[pl.ds(s * NG, NG)], sems.at[4 + s])
        store.start()
        stores.append(store)
    for store in stores:
        store.wait()


def first_stage(x, u, y, d):
    hbm = pl.BlockSpec(memory_space=pltpu.HBM)
    return pl.pallas_call(
        first_kernel,
        in_specs=[hbm] * 4,
        out_specs=hbm,
        out_shape=jax.ShapeDtypeStruct((NS * NG, 2 * NB * ML, T), BF),
        scratch_shapes=[
            pltpu.VMEM(x.shape, BF),
            pltpu.VMEM(u.shape, BF),
            pltpu.VMEM(y.shape, BF),
            pltpu.VMEM(d.shape, BF),
            pltpu.VMEM((2, TILE * 2 * NB, 128), F32),
            pltpu.VMEM((NS, NG, 2 * NB * ML, T), BF),
            pltpu.SemaphoreType.DMA((4 + NS,)),
        ],
        compiler_params=FULL,
        cost_estimate=cost(2**27, 2**21),
    )(x, u, y, d)


def hidden_kernel(at, r, w2, w3, out, g, cut):
    w2 = w2[0]
    w3 = w3[0]
    g2 = g3 = None
    for s in range(NS):
        v = r[s * NG : (s + 1) * NG].astype(F32)
        fm = v[:, :NB].reshape(TILE, T).astype(BF)
        bd = v[:, NB:].reshape(TILE, T).astype(BF)
        w = mm(w2, fm, TN)
        dgated = mm(w3, bd, NN)
        square = w * w
        h = 0.5 + 0.5 * jnp.tanh(w * (C0 * S1 + (C0 * 0.044715 * S1**3) * square))
        gated = ((w * S1) * h).astype(BF)
        bend = w * (2.0 * C0 * S1 + (6.0 * C0 * 0.044715 * S1**3) * square)
        slope = h + (h * (1.0 - h)) * bend
        dpre = ((dgated * S5) * slope).astype(BF)
        down = mm(w3, gated, TN) * S5
        back_up = mm(w2, dpre, NN) * S1
        a2 = mm(fm, dpre, NT)
        a3 = mm(gated, bd, NT)
        g2, g3 = (a2, a3) if g2 is None else (g2 + a2, g3 + a3)
        both = jnp.concatenate([down.reshape(NG, NB, T), back_up.reshape(NG, NB, T)], 1)
        out[s * NG : (s + 1) * NG] = both.astype(BF)
    for c in range(4):
        v = (g2[:, c * 128 : (c + 1) * 128] * S1).reshape(NZ, NS, R, 128)
        for s in range(NS):
            cut[:, s, c * R : (c + 1) * R] = v[:, s]
    cut[:, :, 4 * R :] = (g3 * S5).reshape(NZ, NS, 4 * R, 128)
    for z in range(NZ):
        g[(z % 2) * NS : (z % 2 + 1) * NS, z // 2] = cut[z].astype(BF)


def hidden_stage(at, r, up2, dn1):
    spec = pltpu.PrefetchScalarGridSpec(
        num_scalar_prefetch=1,
        grid=(ML,),
        in_specs=[
            pl.BlockSpec((NS * NG, 2 * NB, T), lambda m, s: (0, m, 0)),
            pl.BlockSpec((1, TILE, HB), lambda m, s: (s[2] * ML + m, 0, 0)),
            pl.BlockSpec((1, HB, TILE), lambda m, s: (s[2] * ML + m, 0, 0)),
        ],
        out_specs=[pl.BlockSpec((NS * NG, 2 * NB, T), lambda m, s: (0, m, 0))]
        + [pl.BlockSpec((2 * NS, NQ, 8 * R, 128), lambda m, s: (0, 0, m, 0))],
        scratch_shapes=[pltpu.VMEM((NZ, NS, 8 * R, 128), F32)],
    )
    return pl.pallas_call(
        hidden_kernel,
        grid_spec=spec,
        out_shape=[pltpu.HBM((NS * NG, 2 * NB * ML, T), BF)]
        + [pltpu.HBM((2 * NS, NQ, 8 * R * ML, 128), BF)],
        compiler_params=PARAMS,
        cost_estimate=cost(2**30, 2**22),
    )(at, r, up2, dn1)


def outer_kernel(r, x, y, u, g23, gin, grads, rows, cut, sem):
    copy = pltpu.make_async_copy(g23, grads.at[:, :, 1], sem)
    copy.start()
    for s in range(NS):
        for h in range(2):
            rows[h, :, s] = r[s * NG : (s + 1) * NG, :, h * 128 : (h + 1) * 128].astype(F32)
    flat = rows.reshape(2, TILE * 2 * NB, 128)

    def pick(j):
        return jnp.concatenate([flat[h, pl.ds(j, TILE, stride=2 * NB), :] for h in range(2)], 1).astype(BF)

    for b in range(NB):
        f = slice(b * TILE, (b + 1) * TILE)
        down, back_up = pick(b), pick(NB + b)
        gin[:, f] = (mm(back_up, u[b], TT) * S1).astype(BF)
        g1 = (mm(x[:, f], back_up, TT) * S1).reshape(NZ, NS, R, TILE)
        g4 = (mm(down, y[:, f], NN) * S1).reshape(NZ, NS, R, TILE)
        for s in range(NS):
            cut[:, s, b * R : (b + 1) * R] = g1[:, s]
            cut[:, s, (NB + b) * R : (NB + b + 1) * R] = g4[:, s]
    for z in range(NZ):
        grads[(z % 2) * NS : (z % 2 + 1) * NS, z // 2, 0] = cut[z].astype(BF)
    copy.wait()


def outer_stage(r, x, y, u, g23):
    return pl.pallas_call(
        outer_kernel,
        in_specs=[pl.BlockSpec(memory_space=pltpu.VMEM)] * 4 + [pl.BlockSpec(memory_space=pltpu.HBM)],
        out_shape=[
            jax.ShapeDtypeStruct((T, NB * TILE), BF),
            jax.ShapeDtypeStruct((2 * NS, NQ, 2, 2 * NB * R, TILE), BF),
        ],
        scratch_shapes=[
            pltpu.VMEM((2, NG, NS, 2 * NB * ML, 128), F32),
            pltpu.VMEM((NZ, NS, 2 * NB * R, TILE), F32),
            pltpu.SemaphoreType.DMA,
        ],
        compiler_params=PARAMS,
        cost_estimate=cost(2**10, 2**10),
    )(r, x, y, u, g23)


def near_kernel(a, out):
    for q in range(NQ):
        v = a[0, q, 0].astype(F32)
        for n in range(1, 2 * NS):
            v = v + a[n, q, 0].astype(F32)
        out[q, 0] = v.astype(BF)
        for s in range(NS):
            out[q, 1 + s] = (a[s, q, 1].astype(F32) + a[NS + s, q, 1].astype(F32)).astype(BF)


def near_stage(a):
    return pl.pallas_call(
        near_kernel,
        out_shape=jax.ShapeDtypeStruct((NQ, 1 + NS, 2 * NB * R, TILE), BF),
        compiler_params=PARAMS,
        cost_estimate=cost(2**10, 2**10),
    )(a)


def choose(sub, options):
    v = options[-1]
    for s in range(len(options) - 2, -1, -1):
        v = jnp.where(sub == s, options[s], v)
    return v


def step(weight, grad, dither):
    noise = GRID * (dither.astype(F32) / 32768.0 - 0.5)
    return (weight - RATE * grad + noise).astype(BF)


def own_rows(sub, block):
    v = block.astype(F32)
    return choose(sub, [v[:, s * R : (s + 1) * R] for s in range(NS)])


def update_kernel(at, a, up1, up2, dn1, dn2, d1, d2, d3, d4, n1, n2, n3, n4):
    sub = at[2]

    def total(i):
        return (a[0, i].astype(F32) + a[1, i].astype(F32)) + (a[2, i].astype(F32) + a[3, i].astype(F32))

    g = total(0).reshape(2, NB, R, TILE)
    n1[...] = step(own_rows(sub, up1[...]), g[0], d1[...])
    n4[...] = step(own_rows(sub, dn2[...]), g[1], d4[...])
    own = own_rows(sub, up2[...])
    for s in range(NS):
        v = total(1 + s)
        for i in range(ML):
            m = s * ML + i
            w = v[i * 8 * R : (i + 1) * 8 * R]
            grad = jnp.concatenate([w[c * R : (c + 1) * R] for c in range(4)], 1)
            n2[m] = step(own[m], grad, d2[m])
            n3[m] = step(dn1[m].astype(F32), w[4 * R :], d3[m])


def update(at, a, up1, up2, dn1, dn2, d1, d2, d3, d4):
    def whole(*shape):
        return pl.BlockSpec(shape, lambda i, s: (0,) * len(shape))

    def far(s):
        return s[0] * 2 + s[1]

    small = whole(NB, R, TILE)
    wide = whole(NB, R, HB)
    large = whole(NB, 4 * R, TILE)
    block = pl.BlockSpec((NB, NS * R, TILE), lambda i, s: (0, far(s), 0))
    spec = pltpu.PrefetchScalarGridSpec(
        num_scalar_prefetch=1,
        grid=(1,),
        in_specs=[
            whole(NQ, 1 + NS, 2 * NB * R, TILE),
            block,
            pl.BlockSpec((NB, NS * R, HB), lambda i, s: (0, far(s), 0)),
            pl.BlockSpec((NB, 4 * R, TILE), lambda i, s: (0, far(s) * NS + s[2], 0)),
            block,
            small,
            wide,
            large,
            small,
        ],
        out_specs=[small, wide, large, small],
    )
    shapes = ((NB, R, TILE), (NB, R, HB), (NB, 4 * R, TILE), (NB, R, TILE))
    return pl.pallas_call(
        update_kernel,
        grid_spec=spec,
        out_shape=[jax.ShapeDtypeStruct(shape, BF) for shape in shapes],
        compiler_params=PARAMS,
        cost_estimate=cost(2**10, 2**10),
    )(at, a, up1, up2, dn1, dn2, d1, d2, d3, d4)


def on_device(x, dy, up1, up2, dn1, dn2, di1, di2, di3, di4):
    at = jnp.stack([lax.axis_index(a) for a in ("fq", "z1", SUB)]).astype(jnp.int32)
    got = exchange(first_stage(x, up1, dy, dn2), GROUP)
    send, g23 = hidden_stage(at, got, up2, dn1)
    gin, grads = outer_stage(exchange(send, GROUP), x, dy, up1, g23)
    grads = exchange(near_stage(exchange(grads, NEAR)), FAR)
    new1, new2, new3, new4 = update(at, grads, up1, up2, dn1, dn2, di1, di2, di3, di4)
    return gin, new1, new2, new3, new4


def solution(mesh):
    dp, mp = mesh.shape["dp"], mesh.shape["mp"]
    fine = Mesh(mesh.devices.reshape(dp // 8, 2, 2, 2, mp), ("fq", "z1", "zl", "yl", "mp"))
    w = P("mp", None, None)
    d = P("mp", DP, None)
    return jax.shard_map(
        on_device,
        mesh=fine,
        in_specs=(P(DP, "mp"), P(DP, "mp"), w, w, w, w, d, d, d, d),
        out_specs=(P(DP, "mp"), d, d, d, d),
        check_vma=False,
    )
```

```python
import math

import jax
import jax.numpy as jnp
from jax import lax
from jax.experimental import pallas as pl
from jax.experimental.pallas import tpu as pltpu
from jax.sharding import Mesh, PartitionSpec as P

TILE = 128
HB = 512
T = 256
NB = 8
NS = 4
NG = 16
NZ = 8
NQ = 4
ML = NB // NS
R = TILE // (NZ * NS)
GRID = 0.25
RATE = 4.0 / math.sqrt(8192)
S1 = TILE ** -0.5
S5 = HB ** -0.5
C0 = math.sqrt(2.0 / math.pi)
BF = jnp.bfloat16
F32 = jnp.float32

DP = ("fq", "z1", "zl", "yl")
SUB = ("zl", "yl")
NEAR = ("z1", "zl", "yl")
FAR = ("fq",)
GROUP = SUB + ("mp",)

NN = (((1,), (0,)), ((), ()))
NT = (((1,), (1,)), ((), ()))
TN = (((0,), (0,)), ((), ()))
TT = (((0,), (1,)), ((), ()))
PARAMS = pltpu.CompilerParams(vmem_limit_bytes=48 << 20)
FULL = pltpu.CompilerParams(vmem_limit_bytes=64 << 20)


def mm(a, b, dims):
    return lax.dot_general(a, b, dims, preferred_element_type=F32)


def exchange(a, axes):
    return lax.all_to_all(a, axes, 0, 0, tiled=True)


def cost(flops, moved):
    return pl.CostEstimate(flops=flops, bytes_accessed=moved, transcendentals=0)


def first_kernel(x_in, u_in, y_in, d_in, out, x, u, y, d, rows, sent, sems):
    pairs = ((x_in, x), (u_in, u), (y_in, y), (d_in, d))
    loads = [pltpu.make_async_copy(a, b, sems.at[i]) for i, (a, b) in enumerate(pairs)]
    for load in loads:
        load.start()
    loads[0].wait()
    loads[1].wait()
    for h in range(2):
        t = slice(h * 128, (h + 1) * 128)
        for b in range(NB):
            f = slice(b * TILE, (b + 1) * TILE)
            rows[h, pl.ds(b, TILE, stride=2 * NB), :] = mm(u[b], x[t, f], TT) * S1
    loads[2].wait()
    loads[3].wait()
    for h in range(2):
        t = slice(h * 128, (h + 1) * 128)
        for b in range(NB):
            f = slice(b * TILE, (b + 1) * TILE)
            rows[h, pl.ds(NB + b, TILE, stride=2 * NB), :] = mm(d[b], y[t, f], NT) * S1
    view = rows.reshape(2, NG, NS, 2 * NB * ML, 128)
    stores = []
    for s in range(NS):
        for h in range(2):
            sent[s, :, :, h * 128 : (h + 1) * 128] = view[h, :, s].astype(BF)
        store = pltpu.make_async_copy(sent.at[s], out.at[pl.ds(s * NG, NG)], sems.at[4 + s])
        store.start()
        stores.append(store)
    for store in stores:
        store.wait()


def first_stage(x, u, y, d):
    hbm = pl.BlockSpec(memory_space=pltpu.HBM)
    return pl.pallas_call(
        first_kernel,
        in_specs=[hbm] * 4,
        out_specs=hbm,
        out_shape=jax.ShapeDtypeStruct((NS * NG, 2 * NB * ML, T), BF),
        scratch_shapes=[
            pltpu.VMEM(x.shape, BF),
            pltpu.VMEM(u.shape, BF),
            pltpu.VMEM(y.shape, BF),
            pltpu.VMEM(d.shape, BF),
            pltpu.VMEM((2, TILE * 2 * NB, 128), F32),
            pltpu.VMEM((NS, NG, 2 * NB * ML, T), BF),
            pltpu.SemaphoreType.DMA((4 + NS,)),
        ],
        compiler_params=FULL,
        cost_estimate=cost(2**27, 2**21),
    )(x, u, y, d)


def hidden_part(r, w2, w3, s):
    v = r[s * NG : (s + 1) * NG].astype(F32)
    fm = v[:, :NB].reshape(TILE, T).astype(BF)
    bd = v[:, NB:].reshape(TILE, T).astype(BF)
    w = mm(w2, fm, TN)
    dgated = mm(w3, bd, NN)
    square = w * w
    h = 0.5 + 0.5 * jnp.tanh(w * (C0 * S1 + (C0 * 0.044715 * S1**3) * square))
    gated = ((w * S1) * h).astype(BF)
    bend = w * (2.0 * C0 * S1 + (6.0 * C0 * 0.044715 * S1**3) * square)
    slope = h + (h * (1.0 - h)) * bend
    dpre = ((dgated * S5) * slope).astype(BF)
    return fm, bd, gated, dpre


def hidden_kernel(at, r, w2, w3, out):
    w2 = w2[0]
    w3 = w3[0]
    for s in range(NS):
        fm, bd, gated, dpre = hidden_part(r, w2, w3, s)
        down = mm(w3, gated, TN) * S5
        back_up = mm(w2, dpre, NN) * S1
        both = jnp.concatenate([down.reshape(NG, NB, T), back_up.reshape(NG, NB, T)], 1)
        out[s * NG : (s + 1) * NG] = both.astype(BF)


def inner_grads_kernel(at, r, w2, w3, g, cut):
    w2 = w2[0]
    w3 = w3[0]
    g2 = g3 = None
    for s in range(NS):
        fm, bd, gated, dpre = hidden_part(r, w2, w3, s)
        a2 = mm(fm, dpre, NT)
        a3 = mm(gated, bd, NT)
        g2, g3 = (a2, a3) if g2 is None else (g2 + a2, g3 + a3)
    for c in range(4):
        v = (g2[:, c * 128 : (c + 1) * 128] * S1).reshape(NZ, NS, R, 128)
        for s in range(NS):
            cut[:, s, c * R : (c + 1) * R] = v[:, s]
    cut[:, :, 4 * R :] = (g3 * S5).reshape(NZ, NS, 4 * R, 128)
    for z in range(NZ):
        g[(z % 2) * NS : (z % 2 + 1) * NS, z // 2] = cut[z].astype(BF)


def hidden_call(kernel, out_spec, out_shape, scratch, at, r, up2, dn1):
    spec = pltpu.PrefetchScalarGridSpec(
        num_scalar_prefetch=1,
        grid=(ML,),
        in_specs=[
            pl.BlockSpec((NS * NG, 2 * NB, T), lambda m, s: (0, m, 0)),
            pl.BlockSpec((1, TILE, HB), lambda m, s: (s[2] * ML + m, 0, 0)),
            pl.BlockSpec((1, HB, TILE), lambda m, s: (s[2] * ML + m, 0, 0)),
        ],
        out_specs=out_spec,
        scratch_shapes=scratch,
    )
    return pl.pallas_call(
        kernel,
        grid_spec=spec,
        out_shape=out_shape,
        compiler_params=PARAMS,
        cost_estimate=cost(2**30, 2**22),
    )(at, r, up2, dn1)


def hidden_stage(*args):
    block = pl.BlockSpec((NS * NG, 2 * NB, T), lambda m, s: (0, m, 0))
    return hidden_call(hidden_kernel, block, pltpu.HBM((NS * NG, 2 * NB * ML, T), BF), [], *args)


def inner_grads(*args):
    block = pl.BlockSpec((2 * NS, NQ, 8 * R, 128), lambda m, s: (0, 0, m, 0))
    shape = pltpu.HBM((2 * NS, NQ, 8 * R * ML, 128), BF)
    return hidden_call(inner_grads_kernel, block, shape, [pltpu.VMEM((NZ, NS, 8 * R, 128), F32)], *args)


def outer_kernel(r, x_in, y_in, u_in, g23, gin, grads, x, y, u, rows, cut, sem, sems):
    loads = [pltpu.make_async_copy(a, b, sems.at[i]) for i, (a, b) in enumerate(((x_in, x), (y_in, y), (u_in, u)))]
    for load in loads:
        load.start()
    copy = pltpu.make_async_copy(g23, grads.at[:, :, 1], sem)
    copy.start()
    for s in range(NS):
        for h in range(2):
            rows[h, :, s] = r[s * NG : (s + 1) * NG, :, h * 128 : (h + 1) * 128].astype(F32)
    flat = rows.reshape(2, TILE * 2 * NB, 128)
    for load in loads:
        load.wait()

    def pick(j):
        return jnp.concatenate([flat[h, pl.ds(j, TILE, stride=2 * NB), :] for h in range(2)], 1).astype(BF)

    for b in range(NB):
        f = slice(b * TILE, (b + 1) * TILE)
        down, back_up = pick(b), pick(NB + b)
        gin[:, f] = (mm(back_up, u[b], TT) * S1).astype(BF)
        g1 = (mm(x[:, f], back_up, TT) * S1).reshape(NZ, NS, R, TILE)
        g4 = (mm(down, y[:, f], NN) * S1).reshape(NZ, NS, R, TILE)
        for s in range(NS):
            cut[:, s, b * R : (b + 1) * R] = g1[:, s]
            cut[:, s, (NB + b) * R : (NB + b + 1) * R] = g4[:, s]
    for z in range(NZ):
        grads[(z % 2) * NS : (z % 2 + 1) * NS, z // 2, 0] = cut[z].astype(BF)
    copy.wait()


def outer_stage(r, x, y, u, g23):
    return pl.pallas_call(
        outer_kernel,
        in_specs=[pl.BlockSpec(memory_space=pltpu.VMEM)] + [pl.BlockSpec(memory_space=pltpu.HBM)] * 4,
        out_shape=[
            jax.ShapeDtypeStruct((T, NB * TILE), BF),
            jax.ShapeDtypeStruct((2 * NS, NQ, 2, 2 * NB * R, TILE), BF),
        ],
        scratch_shapes=[
            pltpu.VMEM(x.shape, BF),
            pltpu.VMEM(y.shape, BF),
            pltpu.VMEM(u.shape, BF),
            pltpu.VMEM((2, NG, NS, 2 * NB * ML, 128), F32),
            pltpu.VMEM((NZ, NS, 2 * NB * R, TILE), F32),
            pltpu.SemaphoreType.DMA,
            pltpu.SemaphoreType.DMA((3,)),
        ],
        compiler_params=FULL,
        cost_estimate=cost(2**10, 2**10),
    )(r, x, y, u, g23)


def near_kernel(a, out):
    for q in range(NQ):
        v = a[0, q, 0].astype(F32)
        for n in range(1, 2 * NS):
            v = v + a[n, q, 0].astype(F32)
        out[q, 0] = v.astype(BF)
        for s in range(NS):
            out[q, 1 + s] = (a[s, q, 1].astype(F32) + a[NS + s, q, 1].astype(F32)).astype(BF)


def near_stage(a):
    return pl.pallas_call(
        near_kernel,
        out_shape=jax.ShapeDtypeStruct((NQ, 1 + NS, 2 * NB * R, TILE), BF),
        compiler_params=PARAMS,
        cost_estimate=cost(2**10, 2**10),
    )(a)


def choose(sub, options):
    v = options[-1]
    for s in range(len(options) - 2, -1, -1):
        v = jnp.where(sub == s, options[s], v)
    return v


def step(weight, grad, dither):
    noise = GRID * (dither.astype(F32) / 32768.0 - 0.5)
    return (weight - RATE * grad + noise).astype(BF)


def own_rows(sub, block):
    v = block.astype(F32)
    return choose(sub, [v[:, s * R : (s + 1) * R] for s in range(NS)])


def update_kernel(at, a, up1, up2, dn1, dn2, d1, d2, d3, d4, n1, n2, n3, n4):
    sub = at[2]

    def total(i):
        return (a[0, i].astype(F32) + a[1, i].astype(F32)) + (a[2, i].astype(F32) + a[3, i].astype(F32))

    g = total(0).reshape(2, NB, R, TILE)
    n1[...] = step(own_rows(sub, up1[...]), g[0], d1[...])
    n4[...] = step(own_rows(sub, dn2[...]), g[1], d4[...])
    own = own_rows(sub, up2[...])
    for s in range(NS):
        v = total(1 + s)
        for i in range(ML):
            m = s * ML + i
            w = v[i * 8 * R : (i + 1) * 8 * R]
            grad = jnp.concatenate([w[c * R : (c + 1) * R] for c in range(4)], 1)
            n2[m] = step(own[m], grad, d2[m])
            n3[m] = step(dn1[m].astype(F32), w[4 * R :], d3[m])


def update(at, a, up1, up2, dn1, dn2, d1, d2, d3, d4):
    def whole(*shape):
        return pl.BlockSpec(shape, lambda i, s: (0,) * len(shape))

    def far(s):
        return s[0] * 2 + s[1]

    small = whole(NB, R, TILE)
    wide = whole(NB, R, HB)
    large = whole(NB, 4 * R, TILE)
    block = pl.BlockSpec((NB, NS * R, TILE), lambda i, s: (0, far(s), 0))
    spec = pltpu.PrefetchScalarGridSpec(
        num_scalar_prefetch=1,
        grid=(1,),
        in_specs=[
            whole(NQ, 1 + NS, 2 * NB * R, TILE),
            block,
            pl.BlockSpec((NB, NS * R, HB), lambda i, s: (0, far(s), 0)),
            pl.BlockSpec((NB, 4 * R, TILE), lambda i, s: (0, far(s) * NS + s[2], 0)),
            block,
            small,
            wide,
            large,
            small,
        ],
        out_specs=[small, wide, large, small],
    )
    shapes = ((NB, R, TILE), (NB, R, HB), (NB, 4 * R, TILE), (NB, R, TILE))
    return pl.pallas_call(
        update_kernel,
        grid_spec=spec,
        out_shape=[jax.ShapeDtypeStruct(shape, BF) for shape in shapes],
        compiler_params=PARAMS,
        cost_estimate=cost(2**10, 2**10),
    )(at, a, up1, up2, dn1, dn2, d1, d2, d3, d4)


def on_device(x, dy, up1, up2, dn1, dn2, di1, di2, di3, di4):
    at = jnp.stack([lax.axis_index(a) for a in ("fq", "z1", SUB)]).astype(jnp.int32)
    got = exchange(first_stage(x, up1, dy, dn2), GROUP)
    send = hidden_stage(at, got, up2, dn1)
    g23 = inner_grads(at, got, up2, dn1)
    gin, grads = outer_stage(exchange(send, GROUP), x, dy, up1, g23)
    grads = exchange(near_stage(exchange(grads, NEAR)), FAR)
    new1, new2, new3, new4 = update(at, grads, up1, up2, dn1, dn2, di1, di2, di3, di4)
    return gin, new1, new2, new3, new4


def solution(mesh):
    dp, mp = mesh.shape["dp"], mesh.shape["mp"]
    fine = Mesh(mesh.devices.reshape(dp // 8, 2, 2, 2, mp), ("fq", "z1", "zl", "yl", "mp"))
    w = P("mp", None, None)
    d = P("mp", DP, None)
    return jax.shard_map(
        on_device,
        mesh=fine,
        in_specs=(P(DP, "mp"), P(DP, "mp"), w, w, w, w, d, d, d, d),
        out_specs=(P(DP, "mp"), d, d, d, d),
        check_vma=False,
    )
```
